32 devices in a mesh: enc: 4 (over y, x), seq: 2 (over core), exp: 4 (over z).
Axes of the slice: x: 2, y: 2, z: 4, core: 2. Of those that a mesh axis runs over, the one named last changes fastest.
Arguments:
- tokens: bfloat16 [4096, 2048], P(('enc', 'seq', 'exp')), may hold values from -6 to 6
- frames: bfloat16 [2048, 1024], P(('enc', 'seq', 'exp')), may hold values from -6 to 6
- w_patch: bfloat16 [1024, 1280], P(None, 'seq'), may hold values from -0.1875 to 0.1875
- w_proj: bfloat16 [1280, 2048], P('seq'), may hold values from -0.15625 to 0.15625
- clip_len: int32 [128], P(('enc', 'seq', 'exp')), may hold values from 1 to 16, as said below
- clip_start: int32 [128], P(('enc', 'seq', 'exp')), may hold values from 0 to 127, as said below
- expert_ids: int32 [4096, 8], P(('enc', 'seq', 'exp')), may hold values from 0 to 15, all different within a row; in each aligned block of 128 rows (0 to 127, 128 to 255, ...) at most 80 rows name the same one
- gate_score: float32 [4096, 8], P(('enc', 'seq', 'exp')), may hold values from 0.05 to 1
- cotangent: bfloat16 [4096, 2048], P(('enc', 'seq', 'exp')), may hold values from -0.29882812 to 0.29882812
- w_gate: bfloat16 [16, 2048, 768], P(('enc', 'exp')), may hold values from -0.125 to 0.125
- w_up: bfloat16 [16, 2048, 768], P(('enc', 'exp')), may hold values from -0.125 to 0.125
- w_down: bfloat16 [16, 768, 2048], P(('enc', 'exp')), may hold values from -0.21875 to 0.21875
Outputs:
- moe_out: bfloat16 [4096, 2048], P(('enc', 'seq', 'exp'))
- score_grad: float32 [4096, 8], P(('enc', 'seq', 'exp'))
The draws below stay inside these ranges and needn't reach their ends.
Inputs may be any that keep to these rules, and one draw needn't show every extreme that they name: `clip_len`: every clip has 1 to 16 rows; in every group of devices that share their seq and exp indices some clip has exactly 16 rows. The clip from the encoder device at enc index e lies inside token rows e * 32 to (e + 1) * 32 - 1 of the receiving device: clip_start + clip_len <= (e + 1) * 32, so clips never share a row. `expert_ids`: among the tokens of one device no expert is named more than 80 times, and in every draw some expert is named exactly 80 times by some device's tokens.
All inputs are finite; a program needn't handle non-finite values.
Results may differ from the reference program's by a relative error of at most 0.0085.
Values may be sent and summed in bfloat16 or wider, within the bound.
A program may use at most 128 MiB of HBM per device.

```python
import math
import jax
import jax.numpy as jnp
import numpy as np
from jax import lax

D = 2048
FF = 768
TOP = 8
AW = 1280
ACAP = 16
TOK_DEV = 128
PIN = 1024
EXPERTS = 16
CAP = 80
AROWS = 2048
TOKENS = 4096
N_ENC = 4
DEVICES = 32


def audio_plan(key):
    base = jax.random.fold_in(key, 4111)
    first, second, third, fourth = jax.random.split(base, 4)
    groups = DEVICES // N_ENC
    shape = (N_ENC, groups, N_ENC)
    lengths = jax.random.randint(first, shape, 1, ACAP + 1)
    pick_source = jax.random.randint(third, (1, groups, 1), 0, N_ENC)
    pick_owner = jax.random.randint(fourth, (1, groups, 1), 0, N_ENC)
    source_index = jnp.arange(N_ENC, dtype=jnp.int32)[:, None, None]
    owner_index = jnp.arange(N_ENC, dtype=jnp.int32)[None, None, :]
    chosen = jnp.logical_and(source_index == pick_source, owner_index == pick_owner)
    lengths = jnp.where(chosen, ACAP, lengths).astype(jnp.int32)
    span = TOK_DEV // N_ENC
    offsets = jax.random.randint(second, shape, 0, span - lengths + 1)
    starts = (source_index * span + offsets).astype(jnp.int32)
    return (lengths.reshape(-1), starts.reshape(-1))


def draw_clip_len(key, part):
    return audio_plan(key)[0]


def draw_clip_start(key, part):
    return audio_plan(key)[1]


def block_scale(rng, shape, shards, low, largest):
    level = 1.0
    for dim, shards_of in shards:
        heights = jax.random.uniform(jax.random.fold_in(jax.random.fold_in(rng, 6), dim), (shards_of,), jnp.float32, low / len(shards), largest / len(shards))
        level = level * jnp.repeat(jnp.exp(heights), shape[dim] // shards_of).reshape((-1,) + (1,) * (len(shape) - 1 - dim))
    return level


def routed_block(stream_key, own, number, rows, amount, top, limit, slope):
    ranking = jax.random.permutation(stream_key, amount)
    packed, common = load_shares(amount, rows * top, limit, slope, True), load_shares(amount, rows * top, limit, slope, False)
    places = jnp.arange(amount)

    def named(sizes, offset_by):
        used = int((sizes > 0).sum())
        fixed = max(1, used // 4)
        shifted = fixed + (places - fixed + offset_by * (used - fixed)) % max(1, amount - fixed)
        return jnp.zeros((amount,), jnp.int32).at[ranking[jnp.where(places < fixed, places, shifted)]].set(jnp.asarray(sizes, jnp.int32))

    sizes = jnp.where(number % 4 == 0, named(packed, number // 4), named(common, number - number // 4 - 1))
    mixed = jax.random.permutation(jax.random.fold_in(own, 3), amount)
    giver, receiver = mixed[0:amount // 2 * 2:2], mixed[1:amount // 2 * 2:2]
    slack = jnp.minimum(sizes[giver] - 1, limit - sizes[receiver]) // 2
    slack = jnp.where((giver == ranking[0]) | (receiver == ranking[0]) | (sizes[receiver] == 0), 0, jnp.maximum(slack, 0))
    shifted = jax.random.randint(jax.random.fold_in(own, 4), (amount // 2,), 0, 1 << 20) % (slack + 1)
    sizes = sizes.at[giver].add(-shifted).at[receiver].add(shifted)
    items = jnp.searchsorted(jnp.cumsum(sizes), jnp.arange(rows * top), side="right").astype(jnp.int32)
    table = items.reshape(top, rows).T
    table = table[jax.random.permutation(jax.random.fold_in(own, 1), rows)]
    offset_by = jax.random.randint(jax.random.fold_in(own, 2), (rows, 1), 0, top)
    return jnp.take_along_axis(table, (jnp.arange(top)[None, :] + offset_by) % top, axis=1)


def load_shares(number_of, total, bound, lean, full):
    weights = [(1 << 20) // math.isqrt(grade ** lean) + 1 for grade in range(1, number_of + 1)]
    largest = bound if full else min(bound, max(-(-total // number_of), total * weights[0] // sum(weights)))
    least = 1 if total - largest >= number_of - 1 else 0
    holding, rest = [largest] + [least] * (number_of - 1), total - largest - least * (number_of - 1)
    while rest > 0:
        movable = [i for i in range(1, number_of) if holding[i] < largest] or [i for i in range(1, number_of) if holding[i] < bound]
        whole, remaining = sum([weights[i] for i in movable]), rest
        for i in movable:
            addition = min(bound - holding[i], max(1, remaining * weights[i] // whole), rest)
            holding[i] = holding[i] + addition
            rest = rest - addition
    return np.array(holding)


def scatter_about(rng, dims, deviation, limit, cuts=(), held_as=jnp.bfloat16):
    drawn = deviation * jax.random.normal(rng, dims, jnp.float32)
    if cuts:
        drawn = drawn * block_scale(rng, dims, cuts, -0.22, 0.18)
    return jnp.clip(drawn, -limit, limit).astype(held_as)


def setup_inputs(seed: int = 0) -> dict:
    streams_of = jax.random.split(jax.random.key(seed), 13)
    tokens = scatter_about(streams_of[0], (TOKENS, D), 1.0, 6.0, ((0, 32),))
    frames = scatter_about(streams_of[1], (AROWS, PIN), 1.0, 6.0, ((0, 32),))
    w_patch = scatter_about(streams_of[2], (PIN, AW), PIN ** -0.5, 0.1875, ((1, 2),))
    w_proj = scatter_about(streams_of[3], (AW, D), AW ** -0.5, 0.15625, ((0, 2),))
    clip_len = draw_clip_len(jax.random.fold_in(streams_of[12], 71), 0)
    clip_start = draw_clip_start(jax.random.fold_in(streams_of[12], 71), 0)
    expert_ids_keys = jax.random.split(jax.random.fold_in(streams_of[6], 1), TOKENS // TOK_DEV)
    expert_ids_turns = jax.random.permutation(jax.random.fold_in(streams_of[6], 3), TOKENS // TOK_DEV)
    expert_ids = jax.vmap(lambda own, number: routed_block(jax.random.fold_in(streams_of[6], 2), own, number, TOK_DEV, EXPERTS, TOP, CAP, 2))(expert_ids_keys, expert_ids_turns).reshape((TOKENS, TOP))
    gate_score = jnp.clip(jnp.exp(math.log(1.0) - 2.9957323 * jax.random.uniform(streams_of[7], (TOKENS, TOP), jnp.float32) ** block_scale(streams_of[7], (TOKENS, TOP), ((0, 32),), -0.2, 0.2)), 0.05, 1.0)
    cotangent = scatter_about(streams_of[8], (TOKENS, D), 0.05, 0.29882812, ((0, 32),))
    w_gate = scatter_about(streams_of[9], (EXPERTS, D, FF), D ** -0.5, 0.125, ((0, 16),))
    w_up = scatter_about(streams_of[10], (EXPERTS, D, FF), D ** -0.5, 0.125, ((0, 16),))
    w_down = scatter_about(streams_of[11], (EXPERTS, FF, D), FF ** -0.5, 0.21875, ((0, 16),))
    return dict(tokens=tokens, frames=frames, w_patch=w_patch, w_proj=w_proj, clip_len=clip_len, clip_start=clip_start, expert_ids=expert_ids, gate_score=gate_score, cotangent=cotangent, w_gate=w_gate, w_up=w_up, w_down=w_down)


def expert_rows(rows, gate_mat, up_mat, down_mat):
    gate_part = jnp.dot(rows, gate_mat, preferred_element_type=jnp.float32)
    up_part = jnp.dot(rows, up_mat, preferred_element_type=jnp.float32)
    active = (jax.nn.silu(gate_part) * up_part).astype(jnp.bfloat16)
    return jnp.dot(active, down_mat, preferred_element_type=jnp.float32).astype(jnp.bfloat16)


def reference(tokens, frames, w_patch, w_proj, clip_len, clip_start, expert_ids, gate_score, cotangent, w_gate, w_up, w_down):
    hidden_audio = jax.nn.gelu(jnp.dot(frames, w_patch, preferred_element_type=jnp.float32), approximate=False).astype(jnp.bfloat16)
    audio_embed = jnp.dot(hidden_audio, w_proj, preferred_element_type=jnp.float32).astype(jnp.bfloat16)
    groups = DEVICES // N_ENC
    lengths = clip_len.reshape(N_ENC, groups, N_ENC)
    starts = clip_start.reshape(N_ENC, groups, N_ENC)
    group_index = jnp.arange(groups, dtype=jnp.int32)[None, :, None]
    owner_index = jnp.arange(N_ENC, dtype=jnp.int32)[None, None, :]
    base = (owner_index * groups + group_index) * TOK_DEV + starts
    offsets = jnp.arange(ACAP, dtype=jnp.int32)
    targets = base[..., None] + offsets
    targets = jnp.where(offsets < lengths[..., None], targets, TOKENS).astype(jnp.int32)
    mixed = tokens.at[targets.reshape(-1)].set(audio_embed.reshape(-1, D), mode="drop")

    block_ids = expert_ids.reshape(DEVICES, TOK_DEV * TOP)
    onehot = (block_ids[..., None] == jnp.arange(EXPERTS, dtype=jnp.int32)).astype(jnp.int32)
    slots = jnp.sum(jnp.cumsum(onehot, axis=1) * onehot, axis=-1) - 1
    table_rows = jnp.arange(DEVICES, dtype=jnp.int32)[:, None] * CAP + slots
    assign = jnp.arange(TOKENS * TOP, dtype=jnp.int32)
    table = jnp.full((EXPERTS, DEVICES * CAP), TOKENS * TOP, jnp.int32)
    table = table.at[block_ids.reshape(-1), table_rows.reshape(-1)].set(assign)

    padded = jnp.concatenate([mixed, jnp.zeros((1, D), jnp.bfloat16)], axis=0)
    cot_pad = jnp.concatenate([cotangent, jnp.zeros((1, D), jnp.bfloat16)], axis=0)
    total = jnp.sum(gate_score, axis=-1, keepdims=True)
    gate = gate_score / total
    gate_pad = jnp.concatenate([gate.reshape(-1), jnp.zeros((1,), jnp.float32)])

    def visit(carry, inputs):
        out_acc, dots = carry
        gate_mat, up_mat, down_mat, rows_of = inputs
        token_of = rows_of // TOP
        result = expert_rows(padded[token_of], gate_mat, up_mat, down_mat).astype(jnp.float32)
        out_acc = out_acc.at[token_of].add(gate_pad[rows_of][:, None] * result)
        dots = dots.at[rows_of].set(jnp.sum(cot_pad[token_of].astype(jnp.float32) * result, axis=-1))
        return (out_acc, dots), None

    start_carry = (jnp.zeros((TOKENS + 1, D), jnp.float32), jnp.zeros((TOKENS * TOP + 1,), jnp.float32))
    (out_acc, dots), _ = lax.scan(visit, start_carry, (w_gate, w_up, w_down, table))
    moe_out = out_acc[:TOKENS].astype(jnp.bfloat16)
    score_dot = dots[:TOKENS * TOP].reshape(TOKENS, TOP)
    score_grad = (score_dot - jnp.sum(gate * score_dot, axis=-1, keepdims=True)) / total
    return moe_out, score_grad
```

```python
import jax
import jax.numpy as jnp
from jax import lax
from jax.sharding import PartitionSpec as P

F32 = jnp.float32
BF16 = jnp.bfloat16


def expert_rows(rows, gate_mat, up_mat, down_mat):
    gate_part = jnp.dot(rows, gate_mat, preferred_element_type=F32)
    up_part = jnp.dot(rows, up_mat, preferred_element_type=F32)
    active = (jax.nn.silu(gate_part) * up_part).astype(BF16)
    return jnp.dot(active, down_mat, preferred_element_type=F32).astype(BF16)


def audio_tokens(tokens, frames, w_patch, w_proj, clip_len, clip_start):
    audio_count = frames.shape[0]
    width = tokens.shape[1]
    tok_count = tokens.shape[0]
    enc_count = lax.axis_size("enc")
    clip_rows = audio_count // enc_count
    grouped = lax.all_gather(frames, "seq", axis=0, tiled=True)
    hidden_cols = jax.nn.gelu(
        jnp.dot(grouped, w_patch, preferred_element_type=F32), approximate=False
    ).astype(BF16)
    embedded = lax.psum_scatter(
        jnp.dot(hidden_cols, w_proj, preferred_element_type=F32),
        "seq",
        scatter_dimension=0,
        tiled=True,
    )
    embedded = embedded.astype(BF16).reshape(enc_count, clip_rows, width)
    arrived = lax.all_to_all(embedded, "enc", split_axis=0, concat_axis=0, tiled=True)
    both = lax.all_to_all(
        jnp.stack([clip_len, clip_start], axis=1), "enc", split_axis=0, concat_axis=0, tiled=True
    )
    lengths, starts = both[:, 0], both[:, 1]
    offsets = jnp.arange(clip_rows, dtype=jnp.int32)
    positions = jnp.where(
        offsets[None, :] < lengths[:, None], starts[:, None] + offsets[None, :], -1
    ).reshape(-1)
    selector = jnp.arange(tok_count, dtype=jnp.int32)[:, None] == positions[None, :]
    placed = jnp.dot(
        selector.astype(BF16), arrived.reshape(-1, width), preferred_element_type=F32
    )
    return jnp.where(jnp.any(selector, axis=1)[:, None], placed.astype(BF16), tokens)


def per_device(
    tokens,
    frames,
    w_patch,
    w_proj,
    clip_len,
    clip_start,
    expert_ids,
    gate_score,
    cotangent,
    w_gate,
    w_up,
    w_down,
):
    width = tokens.shape[1]
    tok_count = tokens.shape[0]
    top_count = expert_ids.shape[1]
    enc_count = lax.axis_size("enc")
    exp_count = lax.axis_size("exp")
    experts = enc_count * exp_count
    capacity = tok_count * top_count * 5 // (4 * experts)
    total = jnp.sum(gate_score, axis=-1, keepdims=True)
    gate = gate_score / total

    expert_axis = jnp.arange(experts, dtype=jnp.int32)[:, None, None]
    chosen = expert_ids.T[None] == expert_axis.transpose(0, 2, 1)
    member = jnp.any(chosen, axis=1)
    earlier = jnp.arange(tok_count)[:, None] < jnp.arange(tok_count)[None, :]
    slot = jnp.dot(member.astype(BF16), earlier.astype(BF16), preferred_element_type=F32)
    slot = jnp.where(member, slot, -1.0)
    weight = jnp.sum(jnp.where(chosen, gate.T[None], 0.0), axis=1)

    me_exp = lax.axis_index("exp")
    info = jnp.stack([slot, weight], axis=0).reshape(2, enc_count, exp_count, tok_count)
    info = info.transpose(2, 0, 1, 3)
    info = lax.all_to_all(info, "exp", split_axis=0, concat_axis=0, tiled=True)
    slot_in, weight_in = info[:, 0], info[:, 1]
    cot_in = lax.all_gather(cotangent, "exp", axis=0)

    mixed = audio_tokens(tokens, frames, w_patch, w_proj, clip_len, clip_start)
    mixed_in = lax.all_gather(mixed, "exp", axis=0)

    place = slot_in[:, :, None, :] == jnp.arange(capacity, dtype=F32)[None, None, :, None]
    outgoing = jnp.einsum(
        "zect,ztd->ezcd", place.astype(BF16), mixed_in, preferred_element_type=F32
    ).astype(BF16)
    received = lax.all_to_all(outgoing, "enc", split_axis=0, concat_axis=0, tiled=True)
    result = expert_rows(
        received.reshape(experts * capacity, width), w_gate[0], w_up[0], w_down[0]
    )
    results = lax.all_to_all(
        result.reshape(enc_count, exp_count, capacity, width),
        "enc",
        split_axis=0,
        concat_axis=0,
        tiled=True,
    )
    spread = jnp.where(place, weight_in[:, :, None, :], 0.0).astype(BF16)
    partial = jnp.einsum("zect,ezcd->ztd", spread, results, preferred_element_type=F32)
    cross = jnp.einsum("ezcd,ztd->zect", results, cot_in, preferred_element_type=F32)
    dots = jnp.sum(jnp.where(place, cross, 0.0), axis=2)
    partial = lax.all_to_all(
        partial.astype(BF16), "exp", split_axis=0, concat_axis=0, tiled=True
    )
    dots = lax.all_to_all(dots, "exp", split_axis=0, concat_axis=0, tiled=True)
    moe_out = jnp.sum(partial.astype(F32), axis=0).astype(BF16)
    dots = dots.transpose(1, 0, 2).reshape(experts, tok_count)
    score_dot = jnp.sum(jnp.where(chosen, dots[:, None, :], 0.0), axis=0).T
    score_grad = (score_dot - jnp.sum(gate * score_dot, axis=-1, keepdims=True)) / total
    return (moe_out, score_grad)


def solution(mesh):
    rows = P(("enc", "seq", "exp"), None)
    line = P(("enc", "seq", "exp"))
    weights = P(("enc", "exp"), None, None)
    in_specs = (
        rows, rows, P(None, "seq"), P("seq", None), line, line, rows, rows, rows,
        weights, weights, weights,
    )
    return jax.shard_map(
        per_device, mesh=mesh, in_specs=in_specs, out_specs=(rows, rows), check_vma=False
    )
```

```python
import functools

import jax
import jax.numpy as jnp
from jax import lax
from jax.experimental import pallas as pl
from jax.experimental.pallas import tpu as pltpu
from jax.sharding import PartitionSpec as P

F32 = jnp.float32
BF16 = jnp.bfloat16


MESH = pl.DeviceIdType.MESH


def partner(me, step, count, way=1):
    if count & (count - 1):
        return lax.rem(me + way * step + count, count)
    out, bit = 0, 1
    while bit < count:
        flip = (step // bit) % 2
        out = out + ((me // bit + flip) % 2) * bit
        bit *= 2
    return out


def tile_of(i, size):
    return pl.ds(pl.multiple_of(i * size, size), size)


def exchange_kernel(
    z_count, e_count, cap,
    mixed_ref, cot_ref, slot_ref, weight_ref, wg_hbm, wu_hbm, wd_hbm,
    out_ref, dots_ref,
    tok, cots, packed, rows, back, part, acc, dot_send, dot_recv, active, wg, wu, wd,
    w_sem, tok_s, tok_r, cot_s, cot_r, pack_s, pack_r, back_s, back_r, part_s, part_r, dot_s, dot_r,
):
    me_z, me_e = lax.axis_index("exp"), lax.axis_index("enc")
    count, width = mixed_ref.shape
    hidden = wg.shape[1]
    items = e_count * cap
    zs = [partner(me_z, k, z_count) for k in range(z_count)]
    es = [partner(me_e, j, e_count) for j in range(e_count)]
    zfrom = [partner(me_z, k, z_count, -1) for k in range(z_count)]
    efrom = [partner(me_e, j, e_count, -1) for j in range(e_count)]

    loads = [
        pltpu.make_async_copy(a, b, w_sem.at[i])
        for i, (a, b) in enumerate(((wg_hbm, wg), (wu_hbm, wu), (wd_hbm, wd)))
    ]
    for load in loads:
        load.start()

    barrier = pltpu.get_barrier_semaphore()
    for z in zs[1:]:
        pl.semaphore_signal(barrier, inc=1, device_id={"exp": z}, device_id_type=MESH)
    for e in es[1:]:
        pl.semaphore_signal(barrier, inc=1, device_id={"enc": e}, device_id_type=MESH)
    pl.semaphore_wait(barrier, z_count + e_count - 2)

    def along_z(src, dst, send, recv, k, z):
        return pltpu.make_async_remote_copy(
            src_ref=src, dst_ref=dst.at[me_z], send_sem=send.at[k], recv_sem=recv.at[me_z],
            device_id={"exp": z}, device_id_type=MESH,
        )

    def landed(dst, recv, c):
        pltpu.make_async_copy(dst.at[c], dst.at[c], recv.at[c]).wait()

    sent = []

    def go(copy):
        copy.start()
        sent.append(copy)

    for k in range(1, z_count):
        go(along_z(mixed_ref, tok, tok_s, tok_r, k, zs[k]))

    def chosen(c, e):
        slots = lax.broadcasted_iota(jnp.int32, (cap, count), 0).astype(F32)
        return slot_ref[c, e] == slots

    def pack(k):
        c = zfrom[k]
        if k:
            landed(tok, tok_r, c)
        for j in list(range(1, e_count)) + [0]:
            e = es[j]
            place = jnp.where(chosen(c, e), 1.0, 0.0).astype(BF16)
            step = 512

            def body(i, _, place=place, j=j, e=e):
                cols = tile_of(i, step)
                source = mixed_ref[:, cols] if k == 0 else tok[c, :, cols]
                piece = jnp.dot(place, source, preferred_element_type=F32).astype(BF16)
                if j:
                    packed[c, e, :, cols] = piece
                else:
                    rows[c, e, :, cols] = piece
                return 0

            lax.fori_loop(0, width // step, body, 0)
            if j:
                go(pltpu.make_async_remote_copy(
                    src_ref=packed.at[c, e], dst_ref=rows.at[c, me_e],
                    send_sem=pack_s.at[c, e], recv_sem=pack_r.at[c, me_e],
                    device_id={"enc": e}, device_id_type=MESH,
                ))

    def work(k):
        c = zfrom[k]
        for j in range(1, e_count):
            e = efrom[j]
            pltpu.make_async_copy(rows.at[c, e], rows.at[c, e], pack_r.at[c, e]).wait()
        if k == 0:
            for load in loads:
                load.wait()

        def up(i, _):
            cols = tile_of(i, 256)
            x = rows[c].reshape(items, width)
            g = jnp.dot(x, wg[:, cols], preferred_element_type=F32)
            u = jnp.dot(x, wu[:, cols], preferred_element_type=F32)
            active[:, cols] = (g / (1.0 + jnp.exp(-g)) * u).astype(BF16)
            return 0

        lax.fori_loop(0, hidden // 256, up, 0)

        def down(i, _):
            cols = tile_of(i, 256)
            y = jnp.dot(active[...], wd[:, cols], preferred_element_type=F32)
            rows[c, :, :, cols] = y.astype(BF16).reshape(e_count, cap, 256)
            return 0

        lax.fori_loop(0, width // 256, down, 0)
        for j in range(1, e_count):
            e = es[j]
            go(pltpu.make_async_remote_copy(
                src_ref=rows.at[c, e], dst_ref=back.at[c, me_e],
                send_sem=back_s.at[c, e], recv_sem=back_r.at[c, me_e],
                device_id={"enc": e}, device_id_type=MESH,
            ))
        back[c, me_e] = rows[c, me_e]

    def combine(k):
        c = zfrom[k]
        for j in range(1, e_count):
            e = efrom[j]
            pltpu.make_async_copy(back.at[c, e], back.at[c, e], back_r.at[c, e]).wait()
        if k:
            landed(cots, cot_r, c)
        place = [chosen(c, e) for e in range(e_count)]
        spread = jnp.concatenate(
            [jnp.where(place[e], weight_ref[c, e], 0.0) for e in range(e_count)], axis=0
        ).astype(BF16)

        def total(i, _):
            cols = tile_of(i, 256)
            y = back[c, :, :, cols].reshape(items, 256)
            s = lax.dot_general(spread, y, (((0,), (0,)), ((), ())), preferred_element_type=F32)
            if k:
                tok[c, :, cols] = s.astype(BF16)
            else:
                acc[:, cols] = s
            return 0

        lax.fori_loop(0, width // 256, total, 0)
        if k:
            go(along_z(tok.at[c], part, part_s, part_r, k, c))
        other = cot_ref[...] if k == 0 else cots[c]
        for e in range(e_count):
            cross = lax.dot_general(
                back[c, e], other, (((1,), (1,)), ((), ())), preferred_element_type=F32
            )
            line = jnp.sum(jnp.where(place[e], cross, 0.0), axis=0, keepdims=True)
            if k:
                dot_send[c, e : e + 1, :] = line
            else:
                dot_recv[c, e : e + 1, :] = line
        if k:
            go(along_z(dot_send.at[c], dot_recv, dot_s, dot_r, k, c))

    for k in range(z_count):
        pack(k)
        if k == z_count - 1:
            for m in range(1, z_count):
                go(along_z(cot_ref, cots, cot_s, cot_r, m, zs[m]))
        if k >= 1:
            work(k - 1)
        if k >= 3:
            combine(k - 3)
    work(z_count - 1)
    for k in range(max(z_count - 3, 0), z_count):
        combine(k)

    for k in range(1, z_count):
        landed(part, part_r, zfrom[k])
        landed(dot_recv, dot_r, zfrom[k])

    def finish(i, _):
        cols = tile_of(i, 256)
        s = acc[:, cols]
        for k in range(1, z_count):
            s = s + part[zfrom[k], :, cols].astype(F32)
        out_ref[:, cols] = s.astype(BF16)
        return 0

    lax.fori_loop(0, width // 256, finish, 0)
    dots_ref[...] = dot_recv[...]
    for copy in sent:
        copy.wait_send()


def exchange(mixed, cot, slot_in, weight_in, w_gate, w_up, w_down, cap):
    z_count, e_count = slot_in.shape[:2]
    count, width = mixed.shape
    hidden = w_gate.shape[1]
    vmem = pl.BlockSpec(memory_space=pltpu.VMEM)
    anywhere = pl.BlockSpec(memory_space=pl.ANY)
    dma = pltpu.SemaphoreType.DMA
    block = pltpu.VMEM((z_count, e_count, cap, width), BF16)
    line = pltpu.VMEM((z_count, count, width), BF16)
    dots = (z_count, e_count, count)
    return pl.pallas_call(
        functools.partial(exchange_kernel, z_count, e_count, cap),
        out_shape=(
            jax.ShapeDtypeStruct((count, width), BF16),
            jax.ShapeDtypeStruct(dots, F32),
        ),
        in_specs=[vmem] * 4 + [anywhere] * 3,
        out_specs=(vmem, vmem),
        scratch_shapes=[
            line, line, block, block, block, line,
            pltpu.VMEM((count, width), F32),
            pltpu.VMEM(dots, F32), pltpu.VMEM(dots, F32),
            pltpu.VMEM((e_count * cap, hidden), BF16),
            pltpu.VMEM(w_gate.shape, BF16), pltpu.VMEM(w_up.shape, BF16), pltpu.VMEM(w_down.shape, BF16),
            dma((3,)), dma((z_count,)), dma((z_count,)), dma((z_count,)), dma((z_count,)),
            dma((z_count, e_count)), dma((z_count, e_count)),
            dma((z_count, e_count)), dma((z_count, e_count)),
            dma((z_count,)), dma((z_count,)), dma((z_count,)), dma((z_count,)),
        ],
        compiler_params=pltpu.CompilerParams(
            collective_id=0, has_side_effects=True, vmem_limit_bytes=60 * 2**20
        ),
    )(mixed, cot, slot_in[:, :, None, :], weight_in[:, :, None, :], w_gate, w_up, w_down)


def audio_tokens(tokens, frames, w_patch, w_proj, clip_len, clip_start):
    audio_count = frames.shape[0]
    width = tokens.shape[1]
    tok_count = tokens.shape[0]
    enc_count = lax.axis_size("enc")
    clip_rows = audio_count // enc_count
    grouped = lax.all_gather(frames, "seq", axis=0, tiled=True)
    hidden_cols = jax.nn.gelu(
        jnp.dot(grouped, w_patch, preferred_element_type=F32), approximate=False
    ).astype(BF16)
    embedded = lax.psum_scatter(
        jnp.dot(hidden_cols, w_proj, preferred_element_type=F32),
        "seq",
        scatter_dimension=0,
        tiled=True,
    )
    embedded = embedded.astype(BF16).reshape(enc_count, clip_rows, width)
    arrived = lax.all_to_all(embedded, "enc", split_axis=0, concat_axis=0, tiled=True)
    both = lax.all_to_all(
        jnp.stack([clip_len, clip_start], axis=1), "enc", split_axis=0, concat_axis=0, tiled=True
    )
    lengths, starts = both[:, 0], both[:, 1]
    offsets = jnp.arange(clip_rows, dtype=jnp.int32)
    positions = jnp.where(
        offsets[None, :] < lengths[:, None], starts[:, None] + offsets[None, :], -1
    ).reshape(-1)
    selector = jnp.arange(tok_count, dtype=jnp.int32)[:, None] == positions[None, :]
    placed = jnp.dot(
        selector.astype(BF16), arrived.reshape(-1, width), preferred_element_type=F32
    )
    return jnp.where(jnp.any(selector, axis=1)[:, None], placed.astype(BF16), tokens)


def per_device(
    tokens,
    frames,
    w_patch,
    w_proj,
    clip_len,
    clip_start,
    expert_ids,
    gate_score,
    cotangent,
    w_gate,
    w_up,
    w_down,
):
    tok_count = tokens.shape[0]
    top_count = expert_ids.shape[1]
    enc_count = lax.axis_size("enc")
    exp_count = lax.axis_size("exp")
    experts = enc_count * exp_count
    capacity = tok_count * top_count * 5 // (4 * experts)
    total = jnp.sum(gate_score, axis=-1, keepdims=True)
    gate = gate_score / total

    expert_axis = jnp.arange(experts, dtype=jnp.int32)[:, None, None]
    chosen = expert_ids.T[None] == expert_axis.transpose(0, 2, 1)
    member = jnp.any(chosen, axis=1)
    earlier = jnp.arange(tok_count)[:, None] < jnp.arange(tok_count)[None, :]
    slot = jnp.dot(member.astype(BF16), earlier.astype(BF16), preferred_element_type=F32)
    slot = jnp.where(member, slot, -1.0)
    weight = jnp.sum(jnp.where(chosen, gate.T[None], 0.0), axis=1)

    info = jnp.stack([slot, weight], axis=0).reshape(2, enc_count, exp_count, tok_count)
    info = info.transpose(2, 0, 1, 3)
    info = lax.all_to_all(info, "exp", split_axis=0, concat_axis=0, tiled=True)
    slot_in, weight_in = info[:, 0], info[:, 1]
    mixed = audio_tokens(tokens, frames, w_patch, w_proj, clip_len, clip_start)
    padded = -(-capacity // 16) * 16
    moe_out, dots = exchange(
        mixed, cotangent, slot_in, weight_in, w_gate[0], w_up[0], w_down[0], padded
    )
    dots = dots.transpose(1, 0, 2).reshape(experts, tok_count)
    score_dot = jnp.sum(jnp.where(chosen, dots[:, None, :], 0.0), axis=0).T
    score_grad = (score_dot - jnp.sum(gate * score_dot, axis=-1, keepdims=True)) / total
    return (moe_out, score_grad)


def solution(mesh):
    rows = P(("enc", "seq", "exp"), None)
    line = P(("enc", "seq", "exp"))
    weights = P(("enc", "exp"), None, None)
    in_specs = (
        rows, rows, P(None, "seq"), P("seq", None), line, line, rows, rows, rows,
        weights, weights, weights,
    )
    return jax.shard_map(
        per_device, mesh=mesh, in_specs=in_specs, out_specs=(rows, rows), check_vma=False
    )
```

```python
import functools

import jax
import jax.numpy as jnp
from jax import lax
from jax.experimental import pallas as pl
from jax.experimental.pallas import tpu as pltpu
from jax.sharding import PartitionSpec as P

F32 = jnp.float32
BF16 = jnp.bfloat16


MESH = pl.DeviceIdType.MESH


def partner(me, step, count, way=1):
    if count & (count - 1):
        return lax.rem(me + way * step + count, count)
    out, bit = 0, 1
    while bit < count:
        flip = (step // bit) % 2
        out = out + ((me // bit + flip) % 2) * bit
        bit *= 2
    return out


def tile_of(i, size):
    return pl.ds(pl.multiple_of(i * size, size), size)


def exchange_kernel(
    z_count, e_count, s_count, cap, clip_rows,
    tok_ref, frames_ref, pos_ref, info_ref, cot_ref, wa_hbm, wb_hbm, wg_hbm, wu_hbm, wd_hbm,
    out_ref, dots_ref,
    tok, cots, packed, rows, back, part, dot_send, dot_recv, active, wg, wu, wd,
    mixed_ref, wa, heard, grouped, share, shares, embedded, arrived, pos, info,
    w_sem, tok_s, tok_r, cot_s, cot_r, pack_s, pack_r, back_s, back_r, part_s, part_r, dot_s, dot_r,
    frame_s, frame_r, share_s, share_r, clip_s, clip_r, pos_s, pos_r, info_s, info_r,
):
    me_z, me_e, me_s = lax.axis_index("exp"), lax.axis_index("enc"), lax.axis_index("seq")
    count, width = mixed_ref.shape
    hidden = wg.shape[1]
    items = e_count * cap
    zs = [partner(me_z, k, z_count) for k in range(z_count)]
    es = [partner(me_e, j, e_count) for j in range(e_count)]
    zfrom = [partner(me_z, k, z_count, -1) for k in range(z_count)]
    ss = [partner(me_s, j, s_count) for j in range(s_count)]
    sfrom = [partner(me_s, j, s_count, -1) for j in range(s_count)]
    efrom = [partner(me_e, j, e_count, -1) for j in range(e_count)]

    units = wb_hbm.shape[0]
    wb = wd.at[pl.ds(0, units)]
    loads = [
        pltpu.make_async_copy(a, b, w_sem.at[i])
        for i, (a, b) in enumerate(
            ((wa_hbm, wa), (wb_hbm, wb), (wg_hbm, wg), (wu_hbm, wu), (wd_hbm, wd))
        )
    ]
    for load in loads[:4]:
        load.start()

    barrier = pltpu.get_barrier_semaphore()
    for z in zs[1:]:
        pl.semaphore_signal(barrier, inc=1, device_id={"exp": z}, device_id_type=MESH)
    for e in es[1:]:
        pl.semaphore_signal(barrier, inc=1, device_id={"enc": e}, device_id_type=MESH)
    for q in ss[1:]:
        pl.semaphore_signal(barrier, inc=1, device_id={"seq": q}, device_id_type=MESH)
    pl.semaphore_wait(barrier, z_count + e_count + s_count - 3)

    def along_z(src, dst, send, recv, k, z):
        return pltpu.make_async_remote_copy(
            src_ref=src, dst_ref=dst.at[me_z], send_sem=send.at[k], recv_sem=recv.at[me_z],
            device_id={"exp": z}, device_id_type=MESH,
        )

    def landed(dst, recv, c):
        pltpu.make_async_copy(dst.at[c], dst.at[c], recv.at[c]).wait()

    sent = []

    def go(copy):
        copy.start()
        sent.append(copy)

    def across(axis, me, src, dst, send, recv, j, to):
        return pltpu.make_async_remote_copy(
            src_ref=src, dst_ref=dst.at[me], send_sem=send.at[j], recv_sem=recv.at[me],
            device_id={axis: to}, device_id_type=MESH,
        )

    for j in range(1, s_count):
        go(across("seq", me_s, frames_ref, grouped, frame_s, frame_r, j, ss[j]))
    for j in range(1, e_count):
        go(across("enc", me_e, pos_ref.at[es[j]], pos, pos_s, pos_r, j, es[j]))
    for k in range(1, z_count):
        go(along_z(info_ref.at[zs[k]], info, info_s, info_r, k, zs[k]))
    early = max(z_count // 2, 1)
    for k in range(1, early + 1):
        if k < z_count:
            go(along_z(cot_ref, cots, cot_s, cot_r, k, zs[k]))
    grouped[me_s] = frames_ref[...]
    pos[me_e] = pos_ref[me_e]
    info[me_z] = info_ref[me_z]
    loads[0].wait()
    for j in range(1, s_count):
        landed(grouped, frame_r, sfrom[j])
    audio = frames_ref.shape[0]
    lines = jnp.dot(
        grouped[...].reshape(s_count * audio, frames_ref.shape[1]), wa[...],
        preferred_element_type=F32,
    )
    lines = (0.5 * lines * (1.0 + lax.erf(lines * (0.5**0.5)))).astype(BF16)
    loads[1].wait()
    heard[...] = lines

    def project(i, _):
        cols = tile_of(i, 256)
        y = jnp.dot(heard[...], wd[:units, cols], preferred_element_type=F32)
        share[:, :, cols] = y.reshape(s_count, audio, 256)
        return 0

    lax.fori_loop(0, width // 256, project, 0)
    loads[4].start()
    for j in range(1, s_count):
        go(across("seq", me_s, share.at[ss[j]], shares, share_s, share_r, j, ss[j]))
    for j in range(1, s_count):
        landed(shares, share_r, sfrom[j])

    def add(i, _):
        cols = tile_of(i, 256)
        y = share[me_s, :, cols]
        for j in range(1, s_count):
            y = y + shares[sfrom[j], :, cols]
        embedded[:, :, cols] = y.astype(BF16).reshape(e_count, clip_rows, 256)
        return 0

    lax.fori_loop(0, width // 256, add, 0)
    for j in range(1, e_count):
        go(across("enc", me_e, embedded.at[es[j]], arrived, clip_s, clip_r, j, es[j]))
    arrived[me_e] = embedded[me_e]
    for j in range(1, e_count):
        landed(pos, pos_r, efrom[j])
    at = jnp.full((1, pos.shape[2]), -1.0, F32)
    for e in range(e_count):
        at = jnp.maximum(at, pos[e])
    line = lax.broadcasted_iota(jnp.int32, (count, pos.shape[2]), 0).astype(F32)
    picked = jnp.where(at == line, 1.0, 0.0)
    taken = jnp.sum(picked, axis=1, keepdims=True)
    picked = picked[:, : e_count * clip_rows].astype(BF16)
    for j in range(1, e_count):
        landed(arrived, clip_r, efrom[j])

    def mix(i, _):
        cols = tile_of(i, 256)
        y = arrived[:, :, cols].reshape(e_count * clip_rows, 256)
        y = jnp.dot(picked, y, preferred_element_type=F32)
        keep = tok_ref[:, cols].astype(F32)
        mixed_ref[:, cols] = jnp.where(taken > 0.0, y, keep).astype(BF16)
        return 0

    lax.fori_loop(0, width // 256, mix, 0)

    for k in range(1, z_count):
        go(along_z(mixed_ref, tok, tok_s, tok_r, k, zs[k]))
    for k in range(1, z_count):
        landed(info, info_r, zfrom[k])

    def chosen(c, e):
        slots = lax.broadcasted_iota(jnp.int32, (cap, count), 0).astype(F32)
        return info[c, e] == slots

    def pack(k):
        c = zfrom[k]
        if k:
            landed(tok, tok_r, c)
        for j in list(range(1, e_count)) + [0]:
            e = es[j]
            place = jnp.where(chosen(c, e), 1.0, 0.0).astype(BF16)
            step = 512

            def body(i, _, place=place, j=j, e=e):
                cols = tile_of(i, step)
                source = mixed_ref[:, cols] if k == 0 else tok[c, :, cols]
                piece = jnp.dot(place, source, preferred_element_type=F32).astype(BF16)
                if j:
                    packed[c, e, :, cols] = piece
                else:
                    rows[c, e, :, cols] = piece
                return 0

            lax.fori_loop(0, width // step, body, 0)
            if j:
                go(pltpu.make_async_remote_copy(
                    src_ref=packed.at[c, e], dst_ref=rows.at[c, me_e],
                    send_sem=pack_s.at[c, e], recv_sem=pack_r.at[c, me_e],
                    device_id={"enc": e}, device_id_type=MESH,
                ))

    def work(k):
        c = zfrom[k]
        for j in range(1, e_count):
            e = efrom[j]
            pltpu.make_async_copy(rows.at[c, e], rows.at[c, e], pack_r.at[c, e]).wait()
        if k == 0:
            for load in loads[2:]:
                load.wait()

        def up(i, _):
            cols = tile_of(i, 256)
            x = rows[c].reshape(items, width)
            g = jnp.dot(x, wg[:, cols], preferred_element_type=F32)
            u = jnp.dot(x, wu[:, cols], preferred_element_type=F32)
            active[:, cols] = (g / (1.0 + jnp.exp(-g)) * u).astype(BF16)
            return 0

        lax.fori_loop(0, hidden // 256, up, 0)

        def down(i, _):
            cols = tile_of(i, 256)
            y = jnp.dot(active[...], wd[:, cols], preferred_element_type=F32)
            rows[c, :, :, cols] = y.astype(BF16).reshape(e_count, cap, 256)
            return 0

        lax.fori_loop(0, width // 256, down, 0)
        for j in range(1, e_count):
            e = es[j]
            go(pltpu.make_async_remote_copy(
                src_ref=rows.at[c, e], dst_ref=back.at[c, me_e],
                send_sem=back_s.at[c, e], recv_sem=back_r.at[c, me_e],
                device_id={"enc": e}, device_id_type=MESH,
            ))
        back[c, me_e] = rows[c, me_e]

    def combine(k):
        c = zfrom[k]
        for j in range(1, e_count):
            e = efrom[j]
            pltpu.make_async_copy(back.at[c, e], back.at[c, e], back_r.at[c, e]).wait()
        if k:
            landed(cots, cot_r, c)
        place = [chosen(c, e) for e in range(e_count)]
        spread = jnp.concatenate(
            [jnp.where(place[e], info[c, e_count + e], 0.0) for e in range(e_count)], axis=0
        ).astype(BF16)

        def total(i, _):
            cols = tile_of(i, 256)
            y = back[c, :, :, cols].reshape(items, 256)
            s = lax.dot_general(spread, y, (((0,), (0,)), ((), ())), preferred_element_type=F32)
            if k:
                tok[c, :, cols] = s.astype(BF16)
            else:
                shares[:, : count // s_count, cols] = s.reshape(s_count, count // s_count, 256)
            return 0

        lax.fori_loop(0, width // 256, total, 0)
        if k:
            go(along_z(tok.at[c], part, part_s, part_r, k, c))
        other = cot_ref[...] if k == 0 else cots[c]
        for e in range(e_count):
            cross = lax.dot_general(
                back[c, e], other, (((1,), (1,)), ((), ())), preferred_element_type=F32
            )
            line = jnp.sum(jnp.where(place[e], cross, 0.0), axis=0, keepdims=True)
            if k:
                dot_send[c, e : e + 1, :] = line
            else:
                dot_recv[c, e : e + 1, :] = line
        if k:
            go(along_z(dot_send.at[c], dot_recv, dot_s, dot_r, k, c))

    for k in range(z_count):
        pack(k)
        if k == z_count - 1:
            for m in range(early + 1, z_count):
                go(along_z(cot_ref, cots, cot_s, cot_r, m, zs[m]))
        if k >= 1:
            work(k - 1)
        if k >= 3:
            combine(k - 3)
    work(z_count - 1)
    for k in range(max(z_count - 3, 0), z_count):
        combine(k)

    for k in range(1, z_count):
        landed(part, part_r, zfrom[k])
        landed(dot_recv, dot_r, zfrom[k])

    def finish(i, _):
        cols = tile_of(i, 256)
        s = shares[:, : count // s_count, cols].reshape(count, 256)
        for k in range(1, z_count):
            s = s + part[zfrom[k], :, cols].astype(F32)
        out_ref[:, cols] = s.astype(BF16)
        return 0

    lax.fori_loop(0, width // 256, finish, 0)
    dots_ref[...] = dot_recv[...]
    for copy in sent:
        copy.wait_send()


def exchange(tokens, frames, pos, info, cot, w_patch, w_proj, w_gate, w_up, w_down, cap):
    z_count, e_count, s_count = (lax.axis_size(a) for a in ("exp", "enc", "seq"))
    count, width = tokens.shape
    audio = frames.shape[0]
    units = w_patch.shape[1]
    clip_rows = audio // e_count
    hidden = w_gate.shape[1]
    vmem = pl.BlockSpec(memory_space=pltpu.VMEM)
    anywhere = pl.BlockSpec(memory_space=pl.ANY)
    dma = pltpu.SemaphoreType.DMA
    block = pltpu.VMEM((z_count, e_count, cap, width), BF16)
    line = pltpu.VMEM((z_count, count, width), BF16)
    dots = (z_count, e_count, count)
    return pl.pallas_call(
        functools.partial(exchange_kernel, z_count, e_count, s_count, cap, clip_rows),
        out_shape=(
            jax.ShapeDtypeStruct((count, width), BF16),
            jax.ShapeDtypeStruct(dots, F32),
        ),
        in_specs=[vmem] * 5 + [anywhere] * 5,
        out_specs=(vmem, vmem),
        scratch_shapes=[
            line, line, block, block, block, line,
            pltpu.VMEM(dots, F32), pltpu.VMEM(dots, F32),
            pltpu.VMEM((e_count * cap, hidden), BF16),
            pltpu.VMEM(w_gate.shape, BF16), pltpu.VMEM(w_up.shape, BF16), pltpu.VMEM(w_down.shape, BF16),
            pltpu.VMEM((count, width), BF16),
            pltpu.VMEM(w_patch.shape, BF16),
            pltpu.VMEM((s_count * audio, units), BF16),
            pltpu.VMEM((s_count,) + frames.shape, BF16),
            pltpu.VMEM((s_count, audio, width), F32), pltpu.VMEM((s_count, audio, width), F32),
            pltpu.VMEM((e_count, clip_rows, width), BF16), pltpu.VMEM((e_count, clip_rows, width), BF16),
            pltpu.VMEM(pos.shape, F32), pltpu.VMEM(info.shape, F32),
            dma((5,)), dma((z_count,)), dma((z_count,)), dma((z_count,)), dma((z_count,)),
            dma((z_count, e_count)), dma((z_count, e_count)),
            dma((z_count, e_count)), dma((z_count, e_count)),
            dma((z_count,)), dma((z_count,)), dma((z_count,)), dma((z_count,)),
            dma((s_count,)), dma((s_count,)), dma((s_count,)), dma((s_count,)),
            dma((e_count,)), dma((e_count,)), dma((e_count,)), dma((e_count,)),
            dma((z_count,)), dma((z_count,)),
        ],
        compiler_params=pltpu.CompilerParams(
            collective_id=0, has_side_effects=True, vmem_limit_bytes=60 * 2**20
        ),
    )(tokens, frames, pos, info, cot, w_patch, w_proj, w_gate, w_up, w_down)


def positions(clip_len, clip_start, clip_rows):
    e_count = clip_len.shape[0]
    lanes = -(-e_count * clip_rows // 128) * 128
    lane = jnp.arange(lanes, dtype=jnp.int32) - lax.axis_index("enc") * clip_rows
    mine = (lane[None, :] >= 0) & (lane[None, :] < clip_len[:, None])
    return jnp.where(mine, clip_start[:, None] + lane[None, :], -1).astype(F32)[:, None, :]


def per_device(
    tokens,
    frames,
    w_patch,
    w_proj,
    clip_len,
    clip_start,
    expert_ids,
    gate_score,
    cotangent,
    w_gate,
    w_up,
    w_down,
):
    tok_count = tokens.shape[0]
    top_count = expert_ids.shape[1]
    enc_count = lax.axis_size("enc")
    exp_count = lax.axis_size("exp")
    experts = enc_count * exp_count
    capacity = tok_count * top_count * 5 // (4 * experts)
    total = jnp.sum(gate_score, axis=-1, keepdims=True)
    gate = gate_score / total

    expert_axis = jnp.arange(experts, dtype=jnp.int32)[:, None, None]
    chosen = expert_ids.T[None] == expert_axis.transpose(0, 2, 1)
    member = jnp.any(chosen, axis=1)
    earlier = jnp.arange(tok_count)[:, None] < jnp.arange(tok_count)[None, :]
    slot = jnp.dot(member.astype(BF16), earlier.astype(BF16), preferred_element_type=F32)
    slot = jnp.where(member, slot, -1.0)
    weight = jnp.sum(jnp.where(chosen, gate.T[None], 0.0), axis=1)

    info = jnp.stack([slot, weight], axis=0).reshape(2, enc_count, exp_count, 1, tok_count)
    info = info.transpose(2, 0, 1, 3, 4).reshape(exp_count, 2 * enc_count, 1, tok_count)
    pos = positions(clip_len, clip_start, frames.shape[0] // enc_count)
    padded = -(-capacity // 16) * 16
    moe_out, dots = exchange(
        tokens, frames, pos, info, cotangent, w_patch, w_proj, w_gate[0], w_up[0], w_down[0], padded
    )
    dots = dots.transpose(1, 0, 2).reshape(experts, tok_count)
    score_dot = jnp.sum(jnp.where(chosen, dots[:, None, :], 0.0), axis=0).T
    score_grad = (score_dot - jnp.sum(gate * score_dot, axis=-1, keepdims=True)) / total
    return (moe_out, score_grad)


def solution(mesh):
    rows = P(("enc", "seq", "exp"), None)
    line = P(("enc", "seq", "exp"))
    weights = P(("enc", "exp"), None, None)
    in_specs = (
        rows, rows, P(None, "seq"), P("seq", None), line, line, rows, rows, rows,
        weights, weights, weights,
    )
    return jax.shard_map(
        per_device, mesh=mesh, in_specs=in_specs, out_specs=(rows, rows), check_vma=False
    )
```

```python
import functools

import jax
import jax.numpy as jnp
from jax import lax
from jax.experimental import pallas as pl
from jax.experimental.pallas import tpu as pltpu
from jax.sharding import PartitionSpec as P

F32 = jnp.float32
BF16 = jnp.bfloat16


MESH = pl.DeviceIdType.MESH


def partner(me, step, count, way=1):
    if count & (count - 1):
        return lax.rem(me + way * step + count, count)
    out, bit = 0, 1
    while bit < count:
        flip = (step // bit) % 2
        out = out + ((me // bit + flip) % 2) * bit
        bit *= 2
    return out


def tile_of(i, size):
    return pl.ds(pl.multiple_of(i * size, size), size)


def exchange_kernel(
    z_count, e_count, s_count, cap, clip_rows,
    tok_ref, frames_ref, pos_ref, info_ref, cot_ref, wa_hbm, wb_hbm, wg_hbm, wu_hbm, wd_hbm,
    out_ref, dots_ref,
    tok, cots, packed, rows, back, part, dot_send, dot_recv, active, wg, wu, wd,
    mixed_ref, wa, heard, grouped, share, shares, embedded, arrived, pos, info,
    w_sem, tok_s, tok_r, cot_s, cot_r, pack_s, pack_r, back_s, back_r, part_s, part_r, dot_s, dot_r,
    frame_s, frame_r, share_s, share_r, clip_s, clip_r, pos_s, pos_r, info_s, info_r,
):
    me_z, me_e, me_s = lax.axis_index("exp"), lax.axis_index("enc"), lax.axis_index("seq")
    count, width = mixed_ref.shape
    hidden = wg.shape[1]
    items = e_count * cap
    zs = [partner(me_z, k, z_count) for k in range(z_count)]
    es = [partner(me_e, j, e_count) for j in range(e_count)]
    zfrom = [partner(me_z, k, z_count, -1) for k in range(z_count)]
    ss = [partner(me_s, j, s_count) for j in range(s_count)]
    sfrom = [partner(me_s, j, s_count, -1) for j in range(s_count)]
    efrom = [partner(me_e, j, e_count, -1) for j in range(e_count)]

    units = wb_hbm.shape[0]
    wb = wd.at[pl.ds(0, units)]
    loads = [
        pltpu.make_async_copy(a, b, w_sem.at[i])
        for i, (a, b) in enumerate(
            ((wa_hbm, wa), (wb_hbm, wb), (wg_hbm, wg), (wu_hbm, wu), (wd_hbm, wd))
        )
    ]
    for load in loads[:4]:
        load.start()

    barrier = pltpu.get_barrier_semaphore()
    for z in zs[1:]:
        pl.semaphore_signal(barrier, inc=1, device_id={"exp": z}, device_id_type=MESH)
    for e in es[1:]:
        pl.semaphore_signal(barrier, inc=1, device_id={"enc": e}, device_id_type=MESH)
    for q in ss[1:]:
        pl.semaphore_signal(barrier, inc=1, device_id={"seq": q}, device_id_type=MESH)
    pl.semaphore_wait(barrier, z_count + e_count + s_count - 3)

    def along_z(src, dst, send, recv, k, z):
        return pltpu.make_async_remote_copy(
            src_ref=src, dst_ref=dst.at[me_z], send_sem=send.at[k], recv_sem=recv.at[me_z],
            device_id={"exp": z}, device_id_type=MESH,
        )

    def landed(dst, recv, c):
        pltpu.make_async_copy(dst.at[c], dst.at[c], recv.at[c]).wait()

    sent = []

    def go(copy):
        copy.start()
        sent.append(copy)

    def across(axis, me, src, dst, send, recv, j, to):
        return pltpu.make_async_remote_copy(
            src_ref=src, dst_ref=dst.at[me], send_sem=send.at[j], recv_sem=recv.at[me],
            device_id={axis: to}, device_id_type=MESH,
        )

    for j in range(1, s_count):
        go(across("seq", me_s, frames_ref, grouped, frame_s, frame_r, j, ss[j]))
    for j in range(1, e_count):
        go(across("enc", me_e, pos_ref.at[es[j]], pos, pos_s, pos_r, j, es[j]))
    for k in range(1, z_count):
        go(along_z(info_ref.at[zs[k]], info, info_s, info_r, k, zs[k]))
    early = max(z_count // 2, 1)
    for k in range(1, early + 1):
        if k < z_count:
            go(along_z(cot_ref, cots, cot_s, cot_r, k, zs[k]))
    grouped[me_s] = frames_ref[...]
    pos[me_e] = pos_ref[me_e]
    info[me_z] = info_ref[me_z]
    loads[0].wait()
    for j in range(1, s_count):
        landed(grouped, frame_r, sfrom[j])
    audio = frames_ref.shape[0]
    lines = jnp.dot(
        grouped[...].reshape(s_count * audio, frames_ref.shape[1]), wa[...],
        preferred_element_type=F32,
    )
    lines = (0.5 * lines * (1.0 + lax.erf(lines * (0.5**0.5)))).astype(BF16)
    loads[1].wait()
    heard[...] = lines

    def project(i, _):
        cols = tile_of(i, 256)
        y = jnp.dot(heard[...], wd[:units, cols], preferred_element_type=F32)
        share[:, :, cols] = y.reshape(s_count, audio, 256)
        return 0

    lax.fori_loop(0, width // 256, project, 0)
    loads[4].start()
    for j in range(1, s_count):
        go(across("seq", me_s, share.at[ss[j]], shares, share_s, share_r, j, ss[j]))
    for j in range(1, s_count):
        landed(shares, share_r, sfrom[j])

    def add(i, _):
        cols = tile_of(i, 256)
        y = share[me_s, :, cols]
        for j in range(1, s_count):
            y = y + shares[sfrom[j], :, cols]
        embedded[:, :, cols] = y.astype(BF16).reshape(e_count, clip_rows, 256)
        return 0

    lax.fori_loop(0, width // 256, add, 0)
    for j in range(1, e_count):
        go(across("enc", me_e, embedded.at[es[j]], arrived, clip_s, clip_r, j, es[j]))
    arrived[me_e] = embedded[me_e]
    for j in range(1, e_count):
        landed(pos, pos_r, efrom[j])
    at = jnp.full((1, pos.shape[2]), -1.0, F32)
    for e in range(e_count):
        at = jnp.maximum(at, pos[e])
    line = lax.broadcasted_iota(jnp.int32, (count, pos.shape[2]), 0).astype(F32)
    picked = jnp.where(at == line, 1.0, 0.0)
    taken = jnp.sum(picked, axis=1, keepdims=True)
    picked = picked[:, : e_count * clip_rows].astype(BF16)
    for j in range(1, e_count):
        landed(arrived, clip_r, efrom[j])

    def mix(i, _):
        cols = tile_of(i, 256)
        y = arrived[:, :, cols].reshape(e_count * clip_rows, 256)
        y = jnp.dot(picked, y, preferred_element_type=F32)
        keep = tok_ref[:, cols].astype(F32)
        mixed_ref[:, cols] = jnp.where(taken > 0.0, y, keep).astype(BF16)
        return 0

    lax.fori_loop(0, width // 256, mix, 0)

    order = [0] + list(range(2, z_count)) + [1]
    for k in order[1:]:
        go(along_z(mixed_ref, tok, tok_s, tok_r, k, zs[k]))
    for k in range(1, z_count):
        landed(info, info_r, zfrom[k])

    def chosen(c, e):
        slots = lax.broadcasted_iota(jnp.int32, (cap, count), 0).astype(F32)
        return info[c, e] == slots

    def pack(k):
        c = zfrom[k]
        if k:
            landed(tok, tok_r, c)
        for j in list(range(1, e_count)) + [0]:
            e = es[j]
            place = jnp.where(chosen(c, e), 1.0, 0.0).astype(BF16)
            step = 512

            def body(i, _, place=place, j=j, e=e):
                cols = tile_of(i, step)
                source = mixed_ref[:, cols] if k == 0 else tok[c, :, cols]
                piece = jnp.dot(place, source, preferred_element_type=F32).astype(BF16)
                if j:
                    packed[c, e, :, cols] = piece
                else:
                    rows[c, e, :, cols] = piece
                return 0

            lax.fori_loop(0, width // step, body, 0)
            if j:
                go(pltpu.make_async_remote_copy(
                    src_ref=packed.at[c, e], dst_ref=rows.at[c, me_e],
                    send_sem=pack_s.at[c, e], recv_sem=pack_r.at[c, me_e],
                    device_id={"enc": e}, device_id_type=MESH,
                ))

    def work(k):
        c = zfrom[k]
        for j in range(1, e_count):
            e = efrom[j]
            pltpu.make_async_copy(rows.at[c, e], rows.at[c, e], pack_r.at[c, e]).wait()
        if k == 0:
            for load in loads[2:]:
                load.wait()

        def up(i, _):
            cols = tile_of(i, 256)
            x = rows[c].reshape(items, width)
            g = jnp.dot(x, wg[:, cols], preferred_element_type=F32)
            u = jnp.dot(x, wu[:, cols], preferred_element_type=F32)
            active[:, cols] = (g / (1.0 + jnp.exp(-g)) * u).astype(BF16)
            return 0

        lax.fori_loop(0, hidden // 256, up, 0)

        def down(i, _):
            cols = tile_of(i, 256)
            y = jnp.dot(active[...], wd[:, cols], preferred_element_type=F32)
            rows[c, :, :, cols] = y.astype(BF16).reshape(e_count, cap, 256)
            return 0

        lax.fori_loop(0, width // 256, down, 0)
        for j in range(1, e_count):
            e = es[j]
            go(pltpu.make_async_remote_copy(
                src_ref=rows.at[c, e], dst_ref=back.at[c, me_e],
                send_sem=back_s.at[c, e], recv_sem=back_r.at[c, me_e],
                device_id={"enc": e}, device_id_type=MESH,
            ))
        back[c, me_e] = rows[c, me_e]

    def combine(k):
        c = zfrom[k]
        for j in range(1, e_count):
            e = efrom[j]
            pltpu.make_async_copy(back.at[c, e], back.at[c, e], back_r.at[c, e]).wait()
        if k:
            landed(cots, cot_r, c)
        place = [chosen(c, e) for e in range(e_count)]
        spread = jnp.concatenate(
            [jnp.where(place[e], info[c, e_count + e], 0.0) for e in range(e_count)], axis=0
        ).astype(BF16)

        def total(i, _):
            cols = tile_of(i, 256)
            y = back[c, :, :, cols].reshape(items, 256)
            s = lax.dot_general(spread, y, (((0,), (0,)), ((), ())), preferred_element_type=F32)
            if k:
                tok[c, :, cols] = s.astype(BF16)
            else:
                shares[:, : count // s_count, cols] = s.reshape(s_count, count // s_count, 256)
            return 0

        lax.fori_loop(0, width // 256, total, 0)
        if k:
            go(along_z(tok.at[c], part, part_s, part_r, k, c))
        other = cot_ref[...] if k == 0 else cots[c]
        for e in range(e_count):
            cross = lax.dot_general(
                back[c, e], other, (((1,), (1,)), ((), ())), preferred_element_type=F32
            )
            line = jnp.sum(jnp.where(place[e], cross, 0.0), axis=0, keepdims=True)
            if k:
                dot_send[c, e : e + 1, :] = line
            else:
                dot_recv[c, e : e + 1, :] = line
        if k:
            go(along_z(dot_send.at[c], dot_recv, dot_s, dot_r, k, c))

    for k in order[:2]:
        pack(k)
        work(k)
    for k in order[2:]:
        pack(k)
    for m in range(early + 1, z_count):
        go(along_z(cot_ref, cots, cot_s, cot_r, m, zs[m]))
    combine(order[0])
    for last, k in zip(order[1:], order[2:]):
        work(k)
        combine(last)
    combine(order[-1])

    for k in range(1, z_count):
        landed(part, part_r, zfrom[k])
        landed(dot_recv, dot_r, zfrom[k])

    def finish(i, _):
        cols = tile_of(i, 256)
        s = shares[:, : count // s_count, cols].reshape(count, 256)
        for k in range(1, z_count):
            s = s + part[zfrom[k], :, cols].astype(F32)
        out_ref[:, cols] = s.astype(BF16)
        return 0

    lax.fori_loop(0, width // 256, finish, 0)
    dots_ref[...] = dot_recv[...]
    for copy in sent:
        copy.wait_send()


def exchange(tokens, frames, pos, info, cot, w_patch, w_proj, w_gate, w_up, w_down, cap):
    z_count, e_count, s_count = (lax.axis_size(a) for a in ("exp", "enc", "seq"))
    count, width = tokens.shape
    audio = frames.shape[0]
    units = w_patch.shape[1]
    clip_rows = audio // e_count
    hidden = w_gate.shape[1]
    vmem = pl.BlockSpec(memory_space=pltpu.VMEM)
    anywhere = pl.BlockSpec(memory_space=pl.ANY)
    dma = pltpu.SemaphoreType.DMA
    block = pltpu.VMEM((z_count, e_count, cap, width), BF16)
    line = pltpu.VMEM((z_count, count, width), BF16)
    dots = (z_count, e_count, count)
    return pl.pallas_call(
        functools.partial(exchange_kernel, z_count, e_count, s_count, cap, clip_rows),
        out_shape=(
            jax.ShapeDtypeStruct((count, width), BF16),
            jax.ShapeDtypeStruct(dots, F32),
        ),
        in_specs=[vmem] * 5 + [anywhere] * 5,
        out_specs=(vmem, vmem),
        scratch_shapes=[
            line, line, block, block, block, line,
            pltpu.VMEM(dots, F32), pltpu.VMEM(dots, F32),
            pltpu.VMEM((e_count * cap, hidden), BF16),
            pltpu.VMEM(w_gate.shape, BF16), pltpu.VMEM(w_up.shape, BF16), pltpu.VMEM(w_down.shape, BF16),
            pltpu.VMEM((count, width), BF16),
            pltpu.VMEM(w_patch.shape, BF16),
            pltpu.VMEM((s_count * audio, units), BF16),
            pltpu.VMEM((s_count,) + frames.shape, BF16),
            pltpu.VMEM((s_count, audio, width), F32), pltpu.VMEM((s_count, audio, width), F32),
            pltpu.VMEM((e_count, clip_rows, width), BF16), pltpu.VMEM((e_count, clip_rows, width), BF16),
            pltpu.VMEM(pos.shape, F32), pltpu.VMEM(info.shape, F32),
            dma((5,)), dma((z_count,)), dma((z_count,)), dma((z_count,)), dma((z_count,)),
            dma((z_count, e_count)), dma((z_count, e_count)),
            dma((z_count, e_count)), dma((z_count, e_count)),
            dma((z_count,)), dma((z_count,)), dma((z_count,)), dma((z_count,)),
            dma((s_count,)), dma((s_count,)), dma((s_count,)), dma((s_count,)),
            dma((e_count,)), dma((e_count,)), dma((e_count,)), dma((e_count,)),
            dma((z_count,)), dma((z_count,)),
        ],
        compiler_params=pltpu.CompilerParams(
            collective_id=0, has_side_effects=True, vmem_limit_bytes=60 * 2**20
        ),
    )(tokens, frames, pos, info, cot, w_patch, w_proj, w_gate, w_up, w_down)


def positions(clip_len, clip_start, clip_rows):
    e_count = clip_len.shape[0]
    lanes = -(-e_count * clip_rows // 128) * 128
    lane = jnp.arange(lanes, dtype=jnp.int32) - lax.axis_index("enc") * clip_rows
    mine = (lane[None, :] >= 0) & (lane[None, :] < clip_len[:, None])
    return jnp.where(mine, clip_start[:, None] + lane[None, :], -1).astype(F32)[:, None, :]


def per_device(
    tokens,
    frames,
    w_patch,
    w_proj,
    clip_len,
    clip_start,
    expert_ids,
    gate_score,
    cotangent,
    w_gate,
    w_up,
    w_down,
):
    tok_count = tokens.shape[0]
    top_count = expert_ids.shape[1]
    enc_count = lax.axis_size("enc")
    exp_count = lax.axis_size("exp")
    experts = enc_count * exp_count
    capacity = tok_count * top_count * 5 // (4 * experts)
    total = jnp.sum(gate_score, axis=-1, keepdims=True)
    gate = gate_score / total

    expert_axis = jnp.arange(experts, dtype=jnp.int32)[:, None, None]
    chosen = expert_ids.T[None] == expert_axis.transpose(0, 2, 1)
    member = jnp.any(chosen, axis=1)
    earlier = jnp.arange(tok_count)[:, None] < jnp.arange(tok_count)[None, :]
    slot = jnp.dot(member.astype(BF16), earlier.astype(BF16), preferred_element_type=F32)
    slot = jnp.where(member, slot, -1.0)
    weight = jnp.sum(jnp.where(chosen, gate.T[None], 0.0), axis=1)

    info = jnp.stack([slot, weight], axis=0).reshape(2, enc_count, exp_count, 1, tok_count)
    info = info.transpose(2, 0, 1, 3, 4).reshape(exp_count, 2 * enc_count, 1, tok_count)
    pos = positions(clip_len, clip_start, frames.shape[0] // enc_count)
    padded = -(-capacity // 16) * 16
    moe_out, dots = exchange(
        tokens, frames, pos, info, cotangent, w_patch, w_proj, w_gate[0], w_up[0], w_down[0], padded
    )
    dots = dots.transpose(1, 0, 2).reshape(experts, tok_count)
    score_dot = jnp.sum(jnp.where(chosen, dots[:, None, :], 0.0), axis=0).T
    score_grad = (score_dot - jnp.sum(gate * score_dot, axis=-1, keepdims=True)) / total
    return (moe_out, score_grad)


def solution(mesh):
    rows = P(("enc", "seq", "exp"), None)
    line = P(("enc", "seq", "exp"))
    weights = P(("enc", "exp"), None, None)
    in_specs = (
        rows, rows, P(None, "seq"), P("seq", None), line, line, rows, rows, rows,
        weights, weights, weights,
    )
    return jax.shard_map(
        per_device, mesh=mesh, in_specs=in_specs, out_specs=(rows, rows), check_vma=False
    )
```
